32 devices in a mesh: row: 4 (over y, core), col: 2 (over x), fsdp: 4 (over z).
Axes of the slice: x: 2, y: 2, z: 4, core: 2. Of those that a mesh axis runs over, the one named last changes fastest.
Arguments:
- master: float32 [4, 2, 96, 4096], P('row', 'col', 'fsdp'), may hold values from -6 to 6
- moment_one: float32 [4, 2, 96, 4096], P('row', 'col', 'fsdp'), may hold values from -3 to 3
- moment_two: float32 [4, 2, 96, 4096], P('row', 'col', 'fsdp'), may hold values from 0.01 to 1
- grads: bfloat16 [4, 2, 96, 4096], P('row', 'col', 'fsdp'), may hold values from -6 to 6
- counts: int32 [4, 2, 8], P('row', 'col'), may hold values from 1 to 4095
- step: int32 [1], replicated, may hold values from 1 to 15
Outputs:
- new_master: float32 [4, 2, 96, 4096], P('row', 'col', 'fsdp')
- new_moment_one: float32 [4, 2, 96, 4096], P('row', 'col', 'fsdp')
- new_moment_two: float32 [4, 2, 96, 4096], P('row', 'col', 'fsdp')
- replica_weights: bfloat16 [4, 2, 4, 96, 4096], P('row', 'col', 'fsdp')
The draws below stay inside these ranges and needn't reach their ends.
All inputs are finite; a program needn't handle non-finite values.
Results may differ from the reference program's by a relative error of at most 0.001.
Values may be sent and summed in bfloat16 or wider, within the bound.
No kernel may reach another device: no remote copies, remote signals or barrier semaphores. Data moves between devices by JAX's collectives and lax.ppermute only.
A program may use at most 64 MiB of HBM per device.

```python
import math
import jax
import jax.numpy as jnp
from jax import lax

D = 4096
BUCKETS = 8
ROWS = 96
N_ROW = 4
N_COL = 2
N_FSDP = 4


def place_ends(entries, own_key, smallest, largest):
    place = [jax.random.randint(jax.random.fold_in(own_key, axis), (), 0, length) for axis, length in enumerate(entries.shape)]
    main_axis = entries.shape.index(max(entries.shape))
    next_to = place[:main_axis] + [(place[main_axis] + 1) % entries.shape[main_axis]] + place[main_axis + 1:]
    return entries.at[tuple(place)].set(smallest).at[tuple(next_to)].set(largest)


def level_of(own_key, shape, pieces, low, largest):
    def one(dim, shards_of):
        steps = jax.random.uniform(jax.random.fold_in(jax.random.fold_in(own_key, 6), dim), (shards_of,), jnp.float32, low / len(pieces), largest / len(pieces))
        return jnp.repeat(jnp.exp(steps), shape[dim] // shards_of).reshape((-1,) + (1,) * (len(shape) - dim - 1))

    loudness = one(*pieces[0])
    for cut in pieces[1:]:
        loudness = loudness * one(*cut)
    return loudness


def scatter_about(own_key, extent, scale, most, cuts=(), kind=jnp.bfloat16):
    entries = jax.random.normal(own_key, extent, jnp.float32) * scale
    if len(cuts) > 0:
        entries = level_of(own_key, extent, cuts, -0.22, 0.18) * entries
    return jnp.clip(entries, min=-most, max=most).astype(kind)


def setup_inputs(seed: int = 0) -> dict:
    key_list = jax.random.split(jax.random.key(seed), 7)
    return {
        "master": scatter_about(key_list[0], (N_ROW, N_COL, ROWS, D), 1.0, 6.0, ((0, 4), (1, 2), (2, 4)), jnp.float32),
        "moment_one": scatter_about(key_list[1], (N_ROW, N_COL, ROWS, D), 0.3, 3.0, ((0, 4), (1, 2), (2, 4)), jnp.float32),
        "moment_two": jnp.clip(jnp.exp(math.log(1.0) - 4.6051702 * jax.random.uniform(key_list[2], (N_ROW, N_COL, ROWS, D), jnp.float32) ** level_of(key_list[2], (N_ROW, N_COL, ROWS, D), ((0, 4), (1, 2), (2, 4)), -0.2, 0.2)), 0.01, 1.0),
        "grads": scatter_about(key_list[3], (N_ROW, N_COL, ROWS, D), 1.0, 6.0, ((0, 4), (1, 2), (2, 4))),
        "counts": place_ends(jax.random.randint(key_list[4], (N_ROW, N_COL, BUCKETS), 1, 4096), jax.random.fold_in(key_list[4], 1), 1, 4095).astype(jnp.int32),
        "step": jax.random.randint(key_list[5], (1,), 1, 16).astype(jnp.int32),
    }


def token_mass(counts):
    lengths = 256.0 * jnp.power(2.0, jnp.arange(BUCKETS).astype(jnp.float32))
    return lax.optimization_barrier(jnp.sum(counts.astype(jnp.float32) * lengths, axis=-1))

def cycle_round(states, weight, axis):
    total = jnp.roll(weight, 1, axis) + weight + jnp.roll(weight, -1, axis)
    scaled_weight = weight[:, :, None, None]
    scaled_total = total[:, :, None, None]
    result = []
    for state in states:
        weighted = scaled_weight * state
        summed = jnp.roll(weighted, 1, axis) + weighted + jnp.roll(weighted, -1, axis)
        result.append(summed / scaled_total)
    return (result, total / 3.0)

def reference(master, moment_one, moment_two, grads, counts, step):
    steps_f = step[0].astype(jnp.float32)
    grad_f = grads.astype(jnp.float32)
    first = 0.9 * moment_one + 0.1 * grad_f
    second = 0.95 * moment_two + 0.05 * grad_f * grad_f
    first_hat = first / (1.0 - jnp.power(jnp.float32(0.9), steps_f))
    second_hat = second / (1.0 - jnp.power(jnp.float32(0.95), steps_f))
    updated = master - 0.1 * (first_hat / (jnp.sqrt(second_hat) + 1e-08) + 0.1 * master)
    weight = token_mass(counts)
    states, mass = cycle_round([updated, first, second], weight, 0)
    states, unused = cycle_round(states, mass, 1)
    new_master, new_first, new_second = states
    rounded = new_master.astype(jnp.bfloat16)
    copies = jnp.broadcast_to(rounded[:, :, None], (N_ROW, N_COL, N_FSDP, ROWS, D))
    return (new_master, new_first, new_second, copies)
```

```python
import functools
import math
import jax
import jax.numpy as jnp
from jax import lax
from jax.experimental import pallas as pl
from jax.experimental.pallas import tpu as pltpu
from jax.sharding import PartitionSpec as P

LANES = 128
STEP = 4 * LANES
SCALE = 32767.0
DIGIT = 1024
COST = dict(c=4_000_000_000, a2=4_000_000_000, b2=4_000_000_000, d=4_000_000_000, a3=0, b3=4_000_000_000, v=0, m=0, ga=0, gb=10000000000, m4=4_000_000_000, pe=2_000_000_000, v4=0, pl=4_000_000_000, t1=2_000_000_000, t2=2_000_000_000, t3=4_000_000_000, gn=0)


def coded(x):
    size = jnp.minimum(jnp.maximum(jnp.abs(x), 1e-30), 16.0)
    root = lax.rsqrt(lax.rsqrt(size)) * (0.5 * SCALE)
    return jnp.round(jnp.where(x < 0, -root, root)).astype(jnp.int32).astype(jnp.int16)


def decoded(code):
    root = code.astype(jnp.int32).astype(jnp.float32) * (2.0 / SCALE)
    square = root * root
    return jnp.where(root < 0, -square, square) * square


def put_weight(ref, weight):
    whole = weight.astype(jnp.int32)
    lane = lax.broadcasted_iota(jnp.int32, whole.shape, 1)
    digits = jnp.where(lane < LANES // 2, lax.shift_right_logical(whole, 10), whole & (DIGIT - 1))
    ref[:, ref.shape[1] - LANES :] = digits.astype(jnp.int16)


def get_weight(ref):
    digits = ref[:, ref.shape[1] - LANES :].astype(jnp.int32).astype(jnp.float32)
    high = jnp.broadcast_to(digits[:, 0:1], digits.shape)
    low = jnp.broadcast_to(digits[:, LANES // 2 : LANES // 2 + 1], digits.shape)
    return high * float(DIGIT) + low


def over_lanes(columns, body):
    step = math.gcd(columns, STEP)

    @pl.loop(0, columns // step)
    def _(j):
        start = pl.multiple_of(j * step, step)
        for q in range(step // LANES):
            body(start + q * LANES)


def lanes(start, offset=0):
    return pl.ds(pl.multiple_of(start + offset, LANES), LANES)


def stepped(master, first, second, fix_first, fix_second):
    ratio = (first * fix_first) / (jnp.sqrt(second * fix_second) + 1e-08)
    return master - 0.1 * (ratio + 0.1 * master)


def first_of(moment_one, grad):
    return 0.9 * moment_one + 0.1 * grad


def second_of(moment_two, grad):
    return 0.95 * moment_two + 0.05 * grad * grad


def early_kernel(master, moment_one, moment_two, grads, counts, step, state, sent, weight_out, fixes, *refs):
    ins, (counts_in, sems) = refs[:4], refs[4:]
    part = state.shape[1]
    low = pl.ds(0, part)
    pairs = [(counts, counts_in)]
    pairs += [(a.at[:, low], b) for a, b in zip((moment_two, grads, moment_one, master), ins)]
    copies = [pltpu.make_async_copy(a, b, sems.at[i]) for i, (a, b) in enumerate(pairs)]
    for copy in copies:
        copy.start()
    copies[0].wait()
    shape = (master.shape[0], LANES)
    many = counts_in[...]
    lengths = lax.shift_left(jnp.ones_like(many), lax.broadcasted_iota(jnp.int32, many.shape, 1))
    total = jnp.sum((many * lengths).astype(jnp.float32), axis=1, keepdims=True)
    weight = jnp.broadcast_to(total, shape)
    weight_out[...] = weight
    put_weight(sent, weight)
    steps = jnp.full(shape, step[0].astype(jnp.float32))
    fix_first = 1.0 / (1.0 - jnp.exp(steps * math.log(0.9)))
    fix_second = 1.0 / (1.0 - jnp.exp(steps * math.log(0.95)))
    fixes[0] = fix_first
    fixes[1] = fix_second
    for copy in copies[1:]:
        copy.wait()
    second_in, grads_in, first_in, master_in = ins

    def body(start):
        at = lanes(start)
        grad = grads_in[:, at].astype(jnp.float32)
        first = first_of(first_in[:, at], grad)
        second = second_of(second_in[:, at], grad)
        new = stepped(master_in[:, at], first, second, fix_first, fix_second)
        state[:, at] = new
        sent[:, at] = coded(new)

    over_lanes(part, body)


def late_kernel(master, moment_one, moment_two, grads, weight, fixes, state, sent):
    part = state.shape[1]
    before = master.shape[1] - part
    put_weight(sent, weight[...])
    fix_first, fix_second = fixes[0], fixes[1]

    def body(start):
        at, high = lanes(start), lanes(start, before)
        grad = grads[:, high].astype(jnp.float32)
        first = first_of(moment_one[:, high], grad)
        second = second_of(moment_two[:, high], grad)
        new = stepped(master[:, high], first, second, fix_first, fix_second)
        state[:, at] = new
        sent[:, at] = coded(new)

    over_lanes(part, body)


def moment_kernel(formula, moment, grads, weight, state, sent):
    put_weight(sent, weight[...])

    def body(start):
        at = lanes(start)
        new = formula(moment[:, at], grads[:, at].astype(jnp.float32))
        state[:, at] = new
        sent[:, at] = coded(new)

    over_lanes(moment.shape[1], body)


def merged(state, own, others, factors):
    weights = [get_weight(own)] + [factor * get_weight(other) for factor, other in zip(factors, others)]
    total = functools.reduce(lax.add, weights)
    shares = [weight / total for weight in weights]

    def at_lanes(at):
        result = shares[0] * state[:, at]
        for share, other in zip(shares[1:], others):
            result = result + share * decoded(other[:, at])
        return result

    return total, at_lanes


def between_kernel(factors, state, own, *refs):
    others, (result, *copies) = refs[: len(factors)], refs[len(factors) :]
    total, at_lanes = merged(state, own, others, factors)
    for sent in copies:
        put_weight(sent, total)

    def body(start):
        at = lanes(start)
        new = at_lanes(at)
        result[:, at] = new
        code = coded(new)
        for sent in copies:
            sent[:, at] = code

    over_lanes(state.shape[1], body)


def last_master_kernel(factors, state, own, *refs):
    others, (result, rounded) = refs[: len(factors)], refs[len(factors) :]
    _, at_lanes = merged(state, own, others, factors)

    def body(start):
        at = lanes(start)
        new = at_lanes(at)
        result[:, at] = new
        rounded[:, at] = new.astype(jnp.bfloat16)

    over_lanes(state.shape[1], body)


def last_late_kernel(factors, state, own, early_rounded, *refs):
    others, (result, rounded, both_rounded) = refs[: len(factors)], refs[len(factors) :]
    _, at_lanes = merged(state, own, others, factors)
    before = early_rounded.shape[1]

    def body(start):
        at, high = lanes(start), lanes(start, before)
        new = at_lanes(at)
        result[:, at] = new
        rounded[:, at] = new.astype(jnp.bfloat16)
        both_rounded[:, high] = new.astype(jnp.bfloat16)

    over_lanes(state.shape[1], body)

    def copy_body(start):
        both_rounded[:, lanes(start)] = early_rounded[:, lanes(start)]

    over_lanes(before, copy_body)


def started(pairs, sems, first=0):
    copies = [pltpu.make_async_copy(a, b, sems.at[first + i]) for i, (a, b) in enumerate(pairs)]
    for copy in copies:
        copy.start()
    return copies


def last_moment(state, own, others, factors, new, result, sems):
    _, at_lanes = merged(state, own, others, factors)
    part = new.shape[1] // 2
    copies = []
    for i in range(2):

        def body(start, base=i * part):
            at = lanes(start, base)
            result[:, at] = at_lanes(at)

        over_lanes(part, body)
        columns = pl.ds(i * part, part)
        copies += started([(result.at[:, columns], new.at[:, columns])], sems, i)
    return copies


def first_moment_kernel(factors, state, own, *refs):
    others, (new, done, result, sems) = refs[: len(factors)], refs[len(factors) :]
    done[...] = jnp.zeros_like(done)
    for copy in last_moment(state, own, others, factors, new, result, sems):
        copy.wait()


def placed(pieces, whole, parts, axis):
    me = lax.axis_index(axis)
    pairs = []
    for part, blocks in zip(parts, pieces):
        pairs += [(block, whole.at[lax.bitwise_xor(me, k), :, part]) for k, block in blocks.items()]
    return pairs


def place_kernel(axis, names, early, late, *refs):
    blocks, (whole, new_master, done, sems) = refs[:-4], refs[-4:]
    done[...] = jnp.zeros_like(done)
    low, high = pl.ds(0, early.shape[1]), pl.ds(early.shape[1], late.shape[1])
    pairs = [(early, new_master.at[:, low]), (late, new_master.at[:, high])]
    pairs += placed(grouped(names, blocks), whole, (pl.ds(0, whole.shape[2]), low, high), axis)
    for copy in started(pairs, sems):
        copy.wait()


def last_kernel(axis, names, factors, size, _, state, own, *refs):
    others, refs = refs[: len(factors)], refs[len(factors) :]
    blocks, (whole, new, result, sems, place_sems) = refs[:-5], refs[-5:]
    low = whole.shape[2] - size
    parts = (pl.ds(0, whole.shape[2]), pl.ds(0, low), pl.ds(low, size))
    copies = started(placed(grouped(names, blocks), whole, parts, axis), place_sems)
    copies += last_moment(state, own, others, factors, new, result, sems)
    for copy in copies:
        copy.wait()


def grouped(names, blocks):
    blocks = iter(blocks)
    return [{k: next(blocks) for k in ks} for ks in names]


def pass_kernel(*_):
    pass


VMEM = pl.BlockSpec(memory_space=pltpu.VMEM)
SMEM = pl.BlockSpec(memory_space=pltpu.SMEM)
HBM = pl.BlockSpec(memory_space=pltpu.HBM)
DONE = ((8, LANES), jnp.float32)


def local(kernel, outs, args, specs=None, out_specs=None, scratch=(), after=(), cost=0, aliases=None):
    specs = specs or [VMEM] * len(args)
    body, skipped = kernel, len(args)

    def ordered_kernel(*refs):
        body(*refs[:skipped], *refs[skipped + len(after) :])

    return pl.pallas_call(
        ordered_kernel if after else kernel,
        out_shape=[jax.ShapeDtypeStruct(shape, kind) for shape, kind in outs],
        in_specs=[*specs, *[pl.BlockSpec(memory_space=pl.ANY)] * len(after)],
        out_specs=out_specs or [VMEM] * len(outs),
        scratch_shapes=scratch,
        input_output_aliases=aliases or {},
        compiler_params=pltpu.CompilerParams(vmem_limit_bytes=24 * 2**20),
        cost_estimate=pl.CostEstimate(flops=cost, bytes_accessed=0, transcendentals=0),
    )(*args, *after)


def along(block, axis, partner):
    return lax.ppermute(block, axis, [(i, partner(i)) for i in range(lax.axis_size(axis))])


def neighbours(block, axis, again=None):
    n = lax.axis_size(axis)
    if n == 2:
        return (2.0,), (along(block, axis, lambda i: i ^ 1),)
    again = block if again is None else again
    if n % 2:
        return (1.0, 1.0), tuple(along(x, axis, lambda i, k=k: (i + k) % n) for k, x in ((1, block), (-1, again)))
    far = along(block, axis, lambda i: (i + 1 if i % 2 else i - 1) % n)
    near = along(again, axis, lambda i: i ^ 1)
    return (1.0, 1.0), (near, far)


def between(state, sent, axis, after=(), cost=0, copies=1):
    factors, others = neighbours(sent, axis)
    outs = [(state.shape, jnp.float32)] + [(sent.shape, jnp.int16)] * copies
    return local(functools.partial(between_kernel, factors), outs, (state, sent, *others), after=after, cost=cost)


def held_until(block, after, cost=0):
    space = [pl.BlockSpec(memory_space=pl.ANY)]
    (same,) = local(pass_kernel, [(block.shape, block.dtype)], [block], space, space, after=after, cost=cost, aliases={0: 0})
    return same


def token_kernel(token):
    token[...] = jnp.zeros_like(token)


def turn(after, cost):
    return local(token_kernel, [DONE], [], [], after=after, cost=cost)


def exchanged(held, axis, far):
    return {**held, **{k ^ far: along(block, axis, lambda i: i ^ far) for k, block in held.items()}}


def per_device(master, moment_one, moment_two, grads, counts, step):
    rows, columns = master.shape[2:]
    n = lax.axis_size("fsdp")
    f32, s16, bf16 = jnp.float32, jnp.int16, jnp.bfloat16
    own = [a.reshape(rows, columns) for a in (master, moment_one, moment_two, grads)]
    low = columns // 2 // LANES * LANES
    full, low_part, high_part = (rows, columns), (rows, low), (rows, columns - low)
    tile = (rows, LANES)

    def with_weight(shape):
        return ((rows, shape[1] + LANES), s16)

    early, sent_early, weight, fixes = local(
        early_kernel,
        [(low_part, f32), with_weight(low_part), (tile, f32), ((2, *tile), f32)],
        [*[pltpu.with_memory_space_constraint(a, pltpu.HBM) for a in (*own, counts.reshape(1, -1))], step],
        [HBM] * 5 + [SMEM],
        scratch=[
            pltpu.VMEM(low_part, f32),
            pltpu.VMEM(low_part, bf16),
            pltpu.VMEM(low_part, f32),
            pltpu.VMEM(low_part, f32),
            pltpu.VMEM((1, counts.shape[2]), jnp.int32),
            pltpu.SemaphoreType.DMA((5,)),
        ],
    )
    late, sent_late = local(
        late_kernel, [(high_part, f32), with_weight(high_part)], [*own, weight, fixes], after=[sent_early]
    )
    first, sent_first = local(
        functools.partial(moment_kernel, first_of),
        [(full, f32), with_weight(full)],
        [own[1], own[3], weight],
        after=[sent_late],
        cost=COST["c"],
    )
    early, sent_early = between(early, sent_early, "row", after=[sent_first], cost=COST["a2"])
    late, sent_late = between(late, sent_late, "row", after=[sent_early], cost=COST["b2"])
    second, sent_second = local(
        functools.partial(moment_kernel, second_of),
        [(full, f32), with_weight(full)],
        [own[2], own[3], weight],
        after=[sent_late],
        cost=COST["d"],
    )

    factors, others = neighbours(sent_early, "col")
    early, rounded_early = local(
        functools.partial(last_master_kernel, factors),
        [(low_part, f32), (low_part, bf16)],
        (early, sent_early, *others),
        after=[sent_second],
        cost=COST["a3"],
    )
    factors, others = neighbours(sent_late, "col")
    late, rounded_late, rounded = local(
        functools.partial(last_late_kernel, factors),
        [(high_part, f32), (high_part, bf16), (full, bf16)],
        (late, sent_late, rounded_early, *others),
        cost=COST["b3"],
    )
    halves = [{0: rounded_early}, {0: rounded_late}]
    far = n // 2
    while far > 1:
        halves = [exchanged(held, "fsdp", far) for held in halves]
        far //= 2
    wholes = exchanged({0: rounded}, "fsdp", 1)

    first, sent_first = between(first, sent_first, "row", after=[rounded], cost=COST["m"])
    second, sent_second, again = between(second, sent_second, "col", after=[sent_first], cost=COST["v"], copies=2)
    halves = [{k: block for k, block in held.items() if k} for held in halves]
    halves[0] = {k: held_until(block, turn([sent_second], COST["t1"]), COST["ga"]) for k, block in halves[0].items()}
    halves[1] = {k: held_until(block, turn(list(halves[0].values()), COST["t2"]), COST["gb"]) for k, block in halves[1].items()}
    again = held_until(again, list(halves[1].values()), COST["gn"])
    halves = [exchanged(held, "fsdp", 1) for held in halves]

    factors, others = neighbours(sent_first, "col")
    new_first, done = local(
        functools.partial(first_moment_kernel, factors),
        [(full, f32), DONE],
        (first, sent_first, *others),
        out_specs=[HBM, VMEM],
        scratch=[pltpu.VMEM(full, f32), pltpu.SemaphoreType.DMA((2,))],
        after=[halves[1][2]],
        cost=COST["m4"],
    )
    sooner = ((0, 1), tuple(range(2, n)), tuple(range(2, n, 2)))
    later = ((), (), tuple(range(3, n, 2)))
    groups = (wholes, *halves)
    blocks = [group[k] for ks, group in zip(sooner, groups) for k in ks]
    whole, new_master, done = local(
        functools.partial(place_kernel, "fsdp", sooner),
        [((n, rows, columns), bf16), (full, f32), DONE],
        (early, late, *blocks),
        out_specs=[HBM, HBM, VMEM],
        scratch=[pltpu.SemaphoreType.DMA((2 + len(blocks),))],
        after=[done],
        cost=COST["pe"],
    )
    factors, others = neighbours(sent_second, "row", again)
    blocks = [group[k] for ks, group in zip(later, groups) for k in ks]
    whole, new_second = local(
        functools.partial(last_kernel, "fsdp", later, factors, columns - low),
        [((n, rows, columns), bf16), (full, f32)],
        (whole, second, sent_second, *others, *blocks),
        [HBM] + [VMEM] * (2 + len(others) + len(blocks)),
        [HBM, HBM],
        scratch=[pltpu.VMEM(full, f32), pltpu.SemaphoreType.DMA((2,)), pltpu.SemaphoreType.DMA((len(blocks),))],
        after=turn([done, *blocks], COST["t3"]),
        cost=COST["v4"],
        aliases={0: 0},
    )
    parts = [a.reshape(master.shape) for a in (new_master, new_first, new_second)]
    return (*parts, whole.reshape(1, 1, 1, n * rows, columns))


def solution(mesh):
    sharded = P("row", "col", "fsdp", None)
    return jax.shard_map(
        per_device,
        mesh=mesh,
        in_specs=(sharded, sharded, sharded, sharded, P("row", "col", None), P()),
        out_specs=(sharded, sharded, sharded, P("row", "col", "fsdp", None, None)),
        check_vma=False,
    )
```

```python
import functools
import math
import jax
import jax.numpy as jnp
from jax import lax
from jax.experimental import pallas as pl
from jax.experimental.pallas import tpu as pltpu
from jax.sharding import PartitionSpec as P

LANES = 128
STEP = 8 * LANES
PARTS = 4
SCALE = 32767.0
DIGIT = 1024
COST = dict(c=4_000_000_000, a2=4_000_000_000, b2=4_000_000_000, d=4_000_000_000, a3=0, b3=4_000_000_000, v=0, m=0, ga=0, gb=10000000000, m4=4_000_000_000, pe=2000000000, v4=0, pl=4_000_000_000, t1=2000000000, t2=2_000_000_000, t3=4_000_000_000, gn=0, t0=40_000_000_000, gz=2000000000)


def coded(x):
    size = jnp.minimum(jnp.maximum(jnp.abs(x), 1e-30), 16.0)
    root = lax.rsqrt(lax.rsqrt(size)) * (0.5 * SCALE)
    return jnp.round(jnp.where(x < 0, -root, root)).astype(jnp.int32).astype(jnp.int16)


def decoded(code):
    root = code.astype(jnp.int32).astype(jnp.float32) * (2.0 / SCALE)
    square = root * root
    return jnp.where(root < 0, -square, square) * square


def put_weight(ref, weight):
    whole = weight.astype(jnp.int32)
    lane = lax.broadcasted_iota(jnp.int32, whole.shape, 1)
    digits = jnp.where(lane < LANES // 2, lax.shift_right_logical(whole, 10), whole & (DIGIT - 1))
    ref[:, ref.shape[1] - LANES :] = digits.astype(jnp.int16)


def get_weight(ref):
    digits = ref[:, ref.shape[1] - LANES :].astype(jnp.int32).astype(jnp.float32)
    high = jnp.broadcast_to(digits[:, 0:1], digits.shape)
    low = jnp.broadcast_to(digits[:, LANES // 2 : LANES // 2 + 1], digits.shape)
    return high * float(DIGIT) + low


def over_lanes(columns, body):
    step = math.gcd(columns, STEP)

    @pl.loop(0, columns // step)
    def _(j):
        start = pl.multiple_of(j * step, step)
        for q in range(step // LANES):
            body(start + q * LANES)


def lanes(start, offset=0):
    return pl.ds(pl.multiple_of(start + offset, LANES), LANES)


def stepped(master, first, second, fix_first, fix_second):
    ratio = (first * fix_first) / (jnp.sqrt(second * fix_second) + 1e-08)
    return master - 0.1 * (ratio + 0.1 * master)


def first_of(moment_one, grad):
    return 0.9 * moment_one + 0.1 * grad


def second_of(moment_two, grad):
    return 0.95 * moment_two + 0.05 * grad * grad


def early_kernel(master, moment_one, moment_two, grads, counts, step, state, sent, weight_out, fixes):
    shape = (master.shape[0], LANES)
    many = counts[...]
    lengths = lax.shift_left(jnp.ones_like(many), lax.broadcasted_iota(jnp.int32, many.shape, 1))
    total = jnp.sum((many * lengths).astype(jnp.float32), axis=1, keepdims=True)
    weight = jnp.broadcast_to(total, shape)
    weight_out[...] = weight
    put_weight(sent, weight)
    steps = jnp.full(shape, step[0].astype(jnp.float32))
    fix_first = 1.0 / (1.0 - jnp.exp(steps * math.log(0.9)))
    fix_second = 1.0 / (1.0 - jnp.exp(steps * math.log(0.95)))
    fixes[0] = fix_first
    fixes[1] = fix_second

    def body(start):
        at = lanes(start)
        grad = grads[:, at].astype(jnp.float32)
        first = first_of(moment_one[:, at], grad)
        second = second_of(moment_two[:, at], grad)
        new = stepped(master[:, at], first, second, fix_first, fix_second)
        state[:, at] = new
        sent[:, at] = coded(new)

    over_lanes(state.shape[1], body)


def late_kernel(master, moment_one, moment_two, grads, weight, fixes, state, sent):
    part = state.shape[1]
    before = master.shape[1] - part
    put_weight(sent, weight[...])
    fix_first, fix_second = fixes[0], fixes[1]

    def body(start):
        at, high = lanes(start), lanes(start, before)
        grad = grads[:, high].astype(jnp.float32)
        first = first_of(moment_one[:, high], grad)
        second = second_of(moment_two[:, high], grad)
        new = stepped(master[:, high], first, second, fix_first, fix_second)
        state[:, at] = new
        sent[:, at] = coded(new)

    over_lanes(part, body)


def moment_kernel(formula, moment, grads, weight, state, sent):
    put_weight(sent, weight[...])

    def body(start):
        at = lanes(start)
        new = formula(moment[:, at], grads[:, at].astype(jnp.float32))
        state[:, at] = new
        sent[:, at] = coded(new)

    over_lanes(moment.shape[1], body)


def merged(state, own, others, factors):
    weights = [get_weight(own)] + [factor * get_weight(other) for factor, other in zip(factors, others)]
    total = functools.reduce(lax.add, weights)
    shares = [weight / total for weight in weights]

    def at_lanes(at):
        result = shares[0] * state[:, at]
        for share, other in zip(shares[1:], others):
            result = result + share * decoded(other[:, at])
        return result

    return total, at_lanes


def between_kernel(factors, state, own, *refs):
    others, (result, *copies) = refs[: len(factors)], refs[len(factors) :]
    total, at_lanes = merged(state, own, others, factors)
    for sent in copies:
        put_weight(sent, total)

    def body(start):
        at = lanes(start)
        new = at_lanes(at)
        result[:, at] = new
        code = coded(new)
        for sent in copies:
            sent[:, at] = code

    over_lanes(state.shape[1], body)


def last_master_kernel(factors, state, own, *refs):
    others, (result, rounded) = refs[: len(factors)], refs[len(factors) :]
    _, at_lanes = merged(state, own, others, factors)

    def body(start):
        at = lanes(start)
        new = at_lanes(at)
        result[:, at] = new
        rounded[:, at] = new.astype(jnp.bfloat16)

    over_lanes(state.shape[1], body)


def last_late_kernel(factors, state, own, early_rounded, *refs):
    others, (result, rounded, both_rounded) = refs[: len(factors)], refs[len(factors) :]
    _, at_lanes = merged(state, own, others, factors)
    before = early_rounded.shape[1]

    def body(start):
        at, high = lanes(start), lanes(start, before)
        new = at_lanes(at)
        result[:, at] = new
        rounded[:, at] = new.astype(jnp.bfloat16)
        both_rounded[:, high] = new.astype(jnp.bfloat16)

    over_lanes(state.shape[1], body)

    def copy_body(start):
        both_rounded[:, lanes(start)] = early_rounded[:, lanes(start)]

    over_lanes(before, copy_body)


def started(pairs, sems, first=0):
    copies = [pltpu.make_async_copy(a, b, sems.at[first + i]) for i, (a, b) in enumerate(pairs)]
    for copy in copies:
        copy.start()
    return copies


def last_moment(state, own, others, factors, new, result, sems):
    _, at_lanes = merged(state, own, others, factors)
    part = new.shape[1] // PARTS
    copies = []
    for i in range(PARTS):

        def body(start, base=i * part):
            at = lanes(start, base)
            result[:, at] = at_lanes(at)

        over_lanes(part, body)
        columns = pl.ds(i * part, part)
        copies += started([(result.at[:, columns], new.at[:, columns])], sems, i)
    return copies


def first_moment_kernel(factors, state, own, *refs):
    others, (new, done, result, sems) = refs[: len(factors)], refs[len(factors) :]
    done[...] = jnp.zeros_like(done)
    for copy in last_moment(state, own, others, factors, new, result, sems):
        copy.wait()


def placed(pieces, whole, parts, axis):
    me = lax.axis_index(axis)
    pairs = []
    for part, blocks in zip(parts, pieces):
        pairs += [(block, whole.at[lax.bitwise_xor(me, k), :, part]) for k, block in blocks.items()]
    return pairs


def place_kernel(axis, names, early, late, *refs):
    blocks, (whole, new_master, done, sems) = refs[:-4], refs[-4:]
    done[...] = jnp.zeros_like(done)
    low, high = pl.ds(0, early.shape[1]), pl.ds(early.shape[1], late.shape[1])
    pairs = [(early, new_master.at[:, low]), (late, new_master.at[:, high])]
    pairs += placed(grouped(names, blocks), whole, (pl.ds(0, whole.shape[2]), low, high), axis)
    for copy in started(pairs, sems):
        copy.wait()


def last_kernel(axis, names, factors, size, _, state, own, *refs):
    others, refs = refs[: len(factors)], refs[len(factors) :]
    blocks, (whole, new, result, sems, place_sems) = refs[:-5], refs[-5:]
    low = whole.shape[2] - size
    parts = (pl.ds(0, whole.shape[2]), pl.ds(0, low), pl.ds(low, size))
    copies = started(placed(grouped(names, blocks), whole, parts, axis), place_sems)
    copies += last_moment(state, own, others, factors, new, result, sems)
    for copy in copies:
        copy.wait()


def grouped(names, blocks):
    blocks = iter(blocks)
    return [{k: next(blocks) for k in ks} for ks in names]


def pass_kernel(*_):
    pass


VMEM = pl.BlockSpec(memory_space=pltpu.VMEM)
SMEM = pl.BlockSpec(memory_space=pltpu.SMEM)
HBM = pl.BlockSpec(memory_space=pltpu.HBM)
DONE = ((8, LANES), jnp.float32)


def local(kernel, outs, args, specs=None, out_specs=None, scratch=(), after=(), cost=0, aliases=None):
    specs = specs or [VMEM] * len(args)
    body, skipped = kernel, len(args)

    def ordered_kernel(*refs):
        body(*refs[:skipped], *refs[skipped + len(after) :])

    return pl.pallas_call(
        ordered_kernel if after else kernel,
        out_shape=[jax.ShapeDtypeStruct(shape, kind) for shape, kind in outs],
        in_specs=[*specs, *[pl.BlockSpec(memory_space=pl.ANY)] * len(after)],
        out_specs=out_specs or [VMEM] * len(outs),
        scratch_shapes=scratch,
        input_output_aliases=aliases or {},
        compiler_params=pltpu.CompilerParams(vmem_limit_bytes=24 * 2**20),
        cost_estimate=pl.CostEstimate(flops=cost, bytes_accessed=0, transcendentals=0),
    )(*args, *after)


def along(block, axis, partner):
    return lax.ppermute(block, axis, [(i, partner(i)) for i in range(lax.axis_size(axis))])


def neighbours(block, axis, again=None):
    n = lax.axis_size(axis)
    if n == 2:
        return (2.0,), (along(block, axis, lambda i: i ^ 1),)
    again = block if again is None else again
    if n % 2:
        return (1.0, 1.0), tuple(along(x, axis, lambda i, k=k: (i + k) % n) for k, x in ((1, block), (-1, again)))
    far = along(block, axis, lambda i: (i + 1 if i % 2 else i - 1) % n)
    near = along(again, axis, lambda i: i ^ 1)
    return (1.0, 1.0), (near, far)


def between(state, sent, axis, after=(), cost=0, copies=1):
    factors, others = neighbours(sent, axis)
    outs = [(state.shape, jnp.float32)] + [(sent.shape, jnp.int16)] * copies
    return local(functools.partial(between_kernel, factors), outs, (state, sent, *others), after=after, cost=cost)


def held_until(block, after, cost=0):
    space = [pl.BlockSpec(memory_space=pl.ANY)]
    (same,) = local(pass_kernel, [(block.shape, block.dtype)], [block], space, space, after=after, cost=cost, aliases={0: 0})
    return same


def token_kernel(token):
    token[...] = jnp.zeros_like(token)


def turn(after, cost):
    return local(token_kernel, [DONE], [], [], after=after, cost=cost)


def exchanged(held, axis, far):
    return {**held, **{k ^ far: along(block, axis, lambda i: i ^ far) for k, block in held.items()}}


def per_device(master, moment_one, moment_two, grads, counts, step):
    rows, columns = master.shape[2:]
    n = lax.axis_size("fsdp")
    f32, s16, bf16 = jnp.float32, jnp.int16, jnp.bfloat16
    own = [a.reshape(rows, columns) for a in (master, moment_one, moment_two, grads)]
    low = columns // 2 // LANES * LANES
    full, low_part, high_part = (rows, columns), (rows, low), (rows, columns - low)
    tile = (rows, LANES)

    def with_weight(shape):
        return ((rows, shape[1] + LANES), s16)

    early, sent_early, weight, fixes = local(
        early_kernel,
        [(low_part, f32), with_weight(low_part), (tile, f32), ((2, *tile), f32)],
        [*own, counts.reshape(1, -1), step],
        [VMEM] * 5 + [SMEM],
        after=turn([], COST["t0"]),
    )
    late, sent_late = local(
        late_kernel, [(high_part, f32), with_weight(high_part)], [*own, weight, fixes], after=[sent_early]
    )
    first, sent_first = local(
        functools.partial(moment_kernel, first_of),
        [(full, f32), with_weight(full)],
        [own[1], own[3], weight],
        after=[sent_late],
        cost=COST["c"],
    )
    early, sent_early = between(early, sent_early, "row", after=[sent_first], cost=COST["a2"])
    late, sent_late = between(late, sent_late, "row", after=[sent_early], cost=COST["b2"])
    second, sent_second = local(
        functools.partial(moment_kernel, second_of),
        [(full, f32), with_weight(full)],
        [own[2], own[3], weight],
        after=[sent_late],
        cost=COST["d"],
    )

    factors, others = neighbours(sent_early, "col")
    early, rounded_early = local(
        functools.partial(last_master_kernel, factors),
        [(low_part, f32), (low_part, bf16)],
        (early, sent_early, *others),
        after=[sent_second],
        cost=COST["a3"],
    )
    factors, others = neighbours(sent_late, "col")
    late, rounded_late, rounded = local(
        functools.partial(last_late_kernel, factors),
        [(high_part, f32), (high_part, bf16), (full, bf16)],
        (late, sent_late, rounded_early, *others),
        cost=COST["b3"],
    )
    halves = [{0: rounded_early}, {0: held_until(rounded_late, [rounded], COST["gz"])}]
    far = n // 2
    while far > 1:
        halves = [exchanged(held, "fsdp", far) for held in halves]
        far //= 2
    wholes = exchanged({0: rounded}, "fsdp", 1)

    first, sent_first = between(first, sent_first, "row", after=[rounded], cost=COST["m"])
    second, sent_second, again = between(second, sent_second, "col", after=[sent_first], cost=COST["v"], copies=2)
    halves = [{k: block for k, block in held.items() if k} for held in halves]
    halves[0] = {k: held_until(block, turn([sent_second], COST["t1"]), COST["ga"]) for k, block in halves[0].items()}
    halves[1] = {k: held_until(block, turn(list(halves[0].values()), COST["t2"]), COST["gb"]) for k, block in halves[1].items()}
    again = held_until(again, list(halves[1].values()), COST["gn"])
    halves = [exchanged(held, "fsdp", 1) for held in halves]

    factors, others = neighbours(sent_first, "col")
    new_first, done = local(
        functools.partial(first_moment_kernel, factors),
        [(full, f32), DONE],
        (first, sent_first, *others),
        out_specs=[HBM, VMEM],
        scratch=[pltpu.VMEM(full, f32), pltpu.SemaphoreType.DMA((PARTS,))],
        after=[halves[1][2]],
        cost=COST["m4"],
    )
    sooner = ((0, 1), tuple(range(2, n)), tuple(range(2, n, 2)))
    later = ((), (), tuple(range(3, n, 2)))
    groups = (wholes, *halves)
    blocks = [group[k] for ks, group in zip(sooner, groups) for k in ks]
    whole, new_master, done = local(
        functools.partial(place_kernel, "fsdp", sooner),
        [((n, rows, columns), bf16), (full, f32), DONE],
        (early, late, *blocks),
        out_specs=[HBM, HBM, VMEM],
        scratch=[pltpu.SemaphoreType.DMA((2 + len(blocks),))],
        after=[done],
        cost=COST["pe"],
    )
    factors, others = neighbours(sent_second, "row", again)
    blocks = [group[k] for ks, group in zip(later, groups) for k in ks]
    whole, new_second = local(
        functools.partial(last_kernel, "fsdp", later, factors, columns - low),
        [((n, rows, columns), bf16), (full, f32)],
        (whole, second, sent_second, *others, *blocks),
        [HBM] + [VMEM] * (2 + len(others) + len(blocks)),
        [HBM, HBM],
        scratch=[pltpu.VMEM(full, f32), pltpu.SemaphoreType.DMA((PARTS,)), pltpu.SemaphoreType.DMA((len(blocks),))],
        after=turn([done, *blocks], COST["t3"]),
        cost=COST["v4"],
        aliases={0: 0},
    )
    parts = [a.reshape(master.shape) for a in (new_master, new_first, new_second)]
    return (*parts, whole.reshape(1, 1, 1, n * rows, columns))


def solution(mesh):
    sharded = P("row", "col", "fsdp", None)
    return jax.shard_map(
        per_device,
        mesh=mesh,
        in_specs=(sharded, sharded, sharded, sharded, P("row", "col", None), P()),
        out_specs=(sharded, sharded, sharded, P("row", "col", "fsdp", None, None)),
        check_vma=False,
    )
```

```python
import functools
import math
import jax
import jax.numpy as jnp
from jax import lax
from jax.experimental import pallas as pl
from jax.experimental.pallas import tpu as pltpu
from jax.sharding import PartitionSpec as P

LANES = 128
STEP = 32 * LANES
PARTS = 4
SCALE = 32767.0
DIGIT = 1024
COST = dict(c=4_000_000_000, a2=4_000_000_000, b2=4_000_000_000, d=4_000_000_000, a3=0, b3=4_000_000_000, v=0, m=0, ga=0, gb=10000000000, m4=4_000_000_000, pe=2000000000, v4=0, pl=4_000_000_000, t1=2000000000, t2=2_000_000_000, t3=4_000_000_000, gn=0, t0=40_000_000_000, gz=2000000000)


def coded(x):
    size = jnp.minimum(jnp.maximum(jnp.abs(x), 1e-30), 16.0)
    root = lax.rsqrt(lax.rsqrt(size)) * (0.5 * SCALE)
    return jnp.round(jnp.where(x < 0, -root, root)).astype(jnp.int32).astype(jnp.int16)


def decoded(code):
    root = code.astype(jnp.int32).astype(jnp.float32) * (2.0 / SCALE)
    square = root * root
    return jnp.where(root < 0, -square, square) * square


def put_weight(ref, weight):
    whole = weight.astype(jnp.int32)
    lane = lax.broadcasted_iota(jnp.int32, whole.shape, 1)
    digits = jnp.where(lane < LANES // 2, lax.shift_right_logical(whole, 10), whole & (DIGIT - 1))
    ref[:, ref.shape[1] - LANES :] = digits.astype(jnp.int16)


def get_weight(ref):
    digits = ref[:, ref.shape[1] - LANES :].astype(jnp.int32).astype(jnp.float32)
    high = jnp.broadcast_to(digits[:, 0:1], digits.shape)
    low = jnp.broadcast_to(digits[:, LANES // 2 : LANES // 2 + 1], digits.shape)
    return high * float(DIGIT) + low


def over_lanes(columns, body):
    step = math.gcd(columns, STEP)

    @pl.loop(0, columns // step)
    def _(j):
        start = pl.multiple_of(j * step, step)
        for q in range(step // LANES):
            body(start + q * LANES)


def lanes(start, offset=0):
    return pl.ds(pl.multiple_of(start + offset, LANES), LANES)


def stepped(master, first, second, fix_first, fix_second):
    ratio = (first * fix_first) / (jnp.sqrt(second * fix_second) + 1e-08)
    return master - 0.1 * (ratio + 0.1 * master)


def first_of(moment_one, grad):
    return 0.9 * moment_one + 0.1 * grad


def second_of(moment_two, grad):
    return 0.95 * moment_two + 0.05 * grad * grad


def early_kernel(master, moment_one, moment_two, grads, counts, step, state, sent, weight_out, fixes):
    shape = (master.shape[0], LANES)
    many = counts[...]
    lengths = lax.shift_left(jnp.ones_like(many), lax.broadcasted_iota(jnp.int32, many.shape, 1))
    total = jnp.sum((many * lengths).astype(jnp.float32), axis=1, keepdims=True)
    weight = jnp.broadcast_to(total, shape)
    weight_out[...] = weight
    put_weight(sent, weight)
    steps = jnp.full(shape, step[0].astype(jnp.float32))
    fix_first = 1.0 / (1.0 - jnp.exp(steps * math.log(0.9)))
    fix_second = 1.0 / (1.0 - jnp.exp(steps * math.log(0.95)))
    fixes[0] = fix_first
    fixes[1] = fix_second

    def body(start):
        at = lanes(start)
        grad = grads[:, at].astype(jnp.float32)
        first = first_of(moment_one[:, at], grad)
        second = second_of(moment_two[:, at], grad)
        new = stepped(master[:, at], first, second, fix_first, fix_second)
        state[:, at] = new
        sent[:, at] = coded(new)

    over_lanes(state.shape[1], body)


def late_kernel(master, moment_one, moment_two, grads, weight, fixes, state, sent):
    part = state.shape[1]
    before = master.shape[1] - part
    put_weight(sent, weight[...])
    fix_first, fix_second = fixes[0], fixes[1]

    def body(start):
        at, high = lanes(start), lanes(start, before)
        grad = grads[:, high].astype(jnp.float32)
        first = first_of(moment_one[:, high], grad)
        second = second_of(moment_two[:, high], grad)
        new = stepped(master[:, high], first, second, fix_first, fix_second)
        state[:, at] = new
        sent[:, at] = coded(new)

    over_lanes(part, body)


def moment_kernel(formula, moment, grads, weight, state, sent):
    put_weight(sent, weight[...])

    def body(start):
        at = lanes(start)
        new = formula(moment[:, at], grads[:, at].astype(jnp.float32))
        state[:, at] = new
        sent[:, at] = coded(new)

    over_lanes(moment.shape[1], body)


def merged(state, own, others, factors):
    weights = [get_weight(own)] + [factor * get_weight(other) for factor, other in zip(factors, others)]
    total = functools.reduce(lax.add, weights)
    shares = [weight / total for weight in weights]

    def at_lanes(at):
        result = shares[0] * state[:, at]
        for share, other in zip(shares[1:], others):
            result = result + share * decoded(other[:, at])
        return result

    return total, at_lanes


def between_kernel(factors, state, own, *refs):
    others, (result, *copies) = refs[: len(factors)], refs[len(factors) :]
    total, at_lanes = merged(state, own, others, factors)
    for sent in copies:
        put_weight(sent, total)

    def body(start):
        at = lanes(start)
        new = at_lanes(at)
        result[:, at] = new
        code = coded(new)
        for sent in copies:
            sent[:, at] = code

    over_lanes(state.shape[1], body)


def last_master_kernel(factors, state, own, *refs):
    others, (result, rounded) = refs[: len(factors)], refs[len(factors) :]
    _, at_lanes = merged(state, own, others, factors)

    def body(start):
        at = lanes(start)
        new = at_lanes(at)
        result[:, at] = new
        rounded[:, at] = new.astype(jnp.bfloat16)

    over_lanes(state.shape[1], body)


def last_late_kernel(factors, state, own, early_rounded, *refs):
    others, (result, rounded, both_rounded) = refs[: len(factors)], refs[len(factors) :]
    _, at_lanes = merged(state, own, others, factors)
    before = early_rounded.shape[1]

    def body(start):
        at, high = lanes(start), lanes(start, before)
        new = at_lanes(at)
        result[:, at] = new
        rounded[:, at] = new.astype(jnp.bfloat16)
        both_rounded[:, high] = new.astype(jnp.bfloat16)

    over_lanes(state.shape[1], body)

    def copy_body(start):
        both_rounded[:, lanes(start)] = early_rounded[:, lanes(start)]

    over_lanes(before, copy_body)


def started(pairs, sems, first=0):
    copies = [pltpu.make_async_copy(a, b, sems.at[first + i]) for i, (a, b) in enumerate(pairs)]
    for copy in copies:
        copy.start()
    return copies


def last_moment(state, own, others, factors, new, result, sems):
    _, at_lanes = merged(state, own, others, factors)
    part = new.shape[1] // PARTS
    copies = []
    for i in range(PARTS):

        def body(start, base=i * part):
            at = lanes(start, base)
            result[:, at] = at_lanes(at)

        over_lanes(part, body)
        columns = pl.ds(i * part, part)
        copies += started([(result.at[:, columns], new.at[:, columns])], sems, i)
    return copies


def first_moment_kernel(factors, state, own, *refs):
    others, (new, done, result, sems) = refs[: len(factors)], refs[len(factors) :]
    done[...] = jnp.zeros_like(done)
    for copy in last_moment(state, own, others, factors, new, result, sems):
        copy.wait()


def placed(pieces, whole, parts, axis):
    me = lax.axis_index(axis)
    pairs = []
    for part, blocks in zip(parts, pieces):
        pairs += [(block, whole.at[lax.bitwise_xor(me, k), :, part]) for k, block in blocks.items()]
    return pairs


def place_kernel(axis, names, early, late, *refs):
    blocks, (whole, new_master, done, sems) = refs[:-4], refs[-4:]
    done[...] = jnp.zeros_like(done)
    low, high = pl.ds(0, early.shape[1]), pl.ds(early.shape[1], late.shape[1])
    pairs = [(early, new_master.at[:, low]), (late, new_master.at[:, high])]
    pairs += placed(grouped(names, blocks), whole, (pl.ds(0, whole.shape[2]), low, high), axis)
    for copy in started(pairs, sems):
        copy.wait()


def last_kernel(axis, names, factors, size, _, state, own, *refs):
    others, refs = refs[: len(factors)], refs[len(factors) :]
    blocks, (whole, new, result, sems, place_sems) = refs[:-5], refs[-5:]
    low = whole.shape[2] - size
    parts = (pl.ds(0, whole.shape[2]), pl.ds(0, low), pl.ds(low, size))
    copies = started(placed(grouped(names, blocks), whole, parts, axis), place_sems)
    copies += last_moment(state, own, others, factors, new, result, sems)
    for copy in copies:
        copy.wait()


def grouped(names, blocks):
    blocks = iter(blocks)
    return [{k: next(blocks) for k in ks} for ks in names]


def pass_kernel(*_):
    pass


VMEM = pl.BlockSpec(memory_space=pltpu.VMEM)
SMEM = pl.BlockSpec(memory_space=pltpu.SMEM)
HBM = pl.BlockSpec(memory_space=pltpu.HBM)
DONE = ((8, LANES), jnp.float32)


def local(kernel, outs, args, specs=None, out_specs=None, scratch=(), after=(), cost=0, aliases=None):
    specs = specs or [VMEM] * len(args)
    body, skipped = kernel, len(args)

    def ordered_kernel(*refs):
        body(*refs[:skipped], *refs[skipped + len(after) :])

    return pl.pallas_call(
        ordered_kernel if after else kernel,
        out_shape=[jax.ShapeDtypeStruct(shape, kind) for shape, kind in outs],
        in_specs=[*specs, *[pl.BlockSpec(memory_space=pl.ANY)] * len(after)],
        out_specs=out_specs or [VMEM] * len(outs),
        scratch_shapes=scratch,
        input_output_aliases=aliases or {},
        compiler_params=pltpu.CompilerParams(vmem_limit_bytes=24 * 2**20),
        cost_estimate=pl.CostEstimate(flops=cost, bytes_accessed=0, transcendentals=0),
    )(*args, *after)


def along(block, axis, partner):
    return lax.ppermute(block, axis, [(i, partner(i)) for i in range(lax.axis_size(axis))])


def neighbours(block, axis, again=None):
    n = lax.axis_size(axis)
    if n == 2:
        return (2.0,), (along(block, axis, lambda i: i ^ 1),)
    again = block if again is None else again
    if n % 2:
        return (1.0, 1.0), tuple(along(x, axis, lambda i, k=k: (i + k) % n) for k, x in ((1, block), (-1, again)))
    far = along(block, axis, lambda i: (i + 1 if i % 2 else i - 1) % n)
    near = along(again, axis, lambda i: i ^ 1)
    return (1.0, 1.0), (near, far)


def between(state, sent, axis, after=(), cost=0, copies=1):
    factors, others = neighbours(sent, axis)
    outs = [(state.shape, jnp.float32)] + [(sent.shape, jnp.int16)] * copies
    return local(functools.partial(between_kernel, factors), outs, (state, sent, *others), after=after, cost=cost)


def held_until(block, after, cost=0):
    space = [pl.BlockSpec(memory_space=pl.ANY)]
    (same,) = local(pass_kernel, [(block.shape, block.dtype)], [block], space, space, after=after, cost=cost, aliases={0: 0})
    return same


def token_kernel(token):
    token[...] = jnp.zeros_like(token)


def turn(after, cost):
    return local(token_kernel, [DONE], [], [], after=after, cost=cost)


def exchanged(held, axis, far):
    return {**held, **{k ^ far: along(block, axis, lambda i: i ^ far) for k, block in held.items()}}


def per_device(master, moment_one, moment_two, grads, counts, step):
    rows, columns = master.shape[2:]
    n = lax.axis_size("fsdp")
    f32, s16, bf16 = jnp.float32, jnp.int16, jnp.bfloat16
    own = [a.reshape(rows, columns) for a in (master, moment_one, moment_two, grads)]
    low = columns // 2 // LANES * LANES
    full, low_part, high_part = (rows, columns), (rows, low), (rows, columns - low)
    tile = (rows, LANES)

    def with_weight(shape):
        return ((rows, shape[1] + LANES), s16)

    early, sent_early, weight, fixes = local(
        early_kernel,
        [(low_part, f32), with_weight(low_part), (tile, f32), ((2, *tile), f32)],
        [*own, counts.reshape(1, -1), step],
        [VMEM] * 5 + [SMEM],
        after=turn([], COST["t0"]),
    )
    late, sent_late = local(
        late_kernel, [(high_part, f32), with_weight(high_part)], [*own, weight, fixes], after=[sent_early]
    )
    first, sent_first = local(
        functools.partial(moment_kernel, first_of),
        [(full, f32), with_weight(full)],
        [own[1], own[3], weight],
        after=[sent_late],
        cost=COST["c"],
    )
    early, sent_early = between(early, sent_early, "row", after=[sent_first], cost=COST["a2"])
    late, sent_late = between(late, sent_late, "row", after=[sent_early], cost=COST["b2"])
    second, sent_second = local(
        functools.partial(moment_kernel, second_of),
        [(full, f32), with_weight(full)],
        [own[2], own[3], weight],
        after=[sent_late],
        cost=COST["d"],
    )

    factors, others = neighbours(sent_early, "col")
    early, rounded_early = local(
        functools.partial(last_master_kernel, factors),
        [(low_part, f32), (low_part, bf16)],
        (early, sent_early, *others),
        after=[sent_second],
        cost=COST["a3"],
    )
    factors, others = neighbours(sent_late, "col")
    late, rounded_late, rounded = local(
        functools.partial(last_late_kernel, factors),
        [(high_part, f32), (high_part, bf16), (full, bf16)],
        (late, sent_late, rounded_early, *others),
        cost=COST["b3"],
    )
    halves = [{0: rounded_early}, {0: held_until(rounded_late, [rounded], COST["gz"])}]
    far = n // 2
    while far > 1:
        halves = [exchanged(held, "fsdp", far) for held in halves]
        far //= 2
    wholes = exchanged({0: rounded}, "fsdp", 1)

    first, sent_first = between(first, sent_first, "row", after=[rounded], cost=COST["m"])
    second, sent_second, again = between(second, sent_second, "col", after=[sent_first], cost=COST["v"], copies=2)
    halves = [{k: block for k, block in held.items() if k} for held in halves]
    halves[0] = {k: held_until(block, turn([sent_second], COST["t1"]), COST["ga"]) for k, block in halves[0].items()}
    halves[1] = {k: held_until(block, turn(list(halves[0].values()), COST["t2"]), COST["gb"]) for k, block in halves[1].items()}
    again = held_until(again, list(halves[1].values()), COST["gn"])
    halves = [exchanged(held, "fsdp", 1) for held in halves]

    factors, others = neighbours(sent_first, "col")
    new_first, done = local(
        functools.partial(first_moment_kernel, factors),
        [(full, f32), DONE],
        (first, sent_first, *others),
        out_specs=[HBM, VMEM],
        scratch=[pltpu.VMEM(full, f32), pltpu.SemaphoreType.DMA((PARTS,))],
        after=[halves[1][2]],
        cost=COST["m4"],
    )
    sooner = ((0, 1), tuple(range(2, n)), tuple(range(2, n, 2)))
    later = ((), (), tuple(range(3, n, 2)))
    groups = (wholes, *halves)
    blocks = [group[k] for ks, group in zip(sooner, groups) for k in ks]
    whole, new_master, done = local(
        functools.partial(place_kernel, "fsdp", sooner),
        [((n, rows, columns), bf16), (full, f32), DONE],
        (early, late, *blocks),
        out_specs=[HBM, HBM, VMEM],
        scratch=[pltpu.SemaphoreType.DMA((2 + len(blocks),))],
        after=[done],
        cost=COST["pe"],
    )
    factors, others = neighbours(sent_second, "row", again)
    blocks = [group[k] for ks, group in zip(later, groups) for k in ks]
    whole, new_second = local(
        functools.partial(last_kernel, "fsdp", later, factors, columns - low),
        [((n, rows, columns), bf16), (full, f32)],
        (whole, second, sent_second, *others, *blocks),
        [HBM] + [VMEM] * (2 + len(others) + len(blocks)),
        [HBM, HBM],
        scratch=[pltpu.VMEM(full, f32), pltpu.SemaphoreType.DMA((PARTS,)), pltpu.SemaphoreType.DMA((len(blocks),))],
        after=turn([done, *blocks], COST["t3"]),
        cost=COST["v4"],
        aliases={0: 0},
    )
    parts = [a.reshape(master.shape) for a in (new_master, new_first, new_second)]
    return (*parts, whole.reshape(1, 1, 1, n * rows, columns))


def solution(mesh):
    sharded = P("row", "col", "fsdp", None)
    return jax.shard_map(
        per_device,
        mesh=mesh,
        in_specs=(sharded, sharded, sharded, sharded, P("row", "col", None), P()),
        out_specs=(sharded, sharded, sharded, P("row", "col", "fsdp", None, None)),
        check_vma=False,
    )
```
